256 devices in a mesh: dp: 8 (over x, y_hi), tensor: 32 (over z, y_lo, core).
Axes of the slice: x: 4, y: 4 (y_hi: 2, y_lo: 2; y = y_hi * 2 + y_lo), z: 8, core: 2. Of those that a mesh axis runs over, the one named last changes fastest.
Arguments:
- x_stash: bfloat16 [3072, 4096], P(('dp', 'tensor')), may hold values from -4 to 4
- x_scale: bfloat16 [3072], P(('dp', 'tensor')), may hold values from 0.29882812 to 3
- grad_out: bfloat16 [3072, 4096], P(('dp', 'tensor')), may hold values from -6 to 6
- w_gate: bfloat16 [4096, 14336], P(None, 'tensor'), may hold values from -0.09375 to 0.09375
- w_up: bfloat16 [4096, 14336], P(None, 'tensor'), may hold values from -0.09375 to 0.09375
- w_down: bfloat16 [14336, 4096], P('tensor'), may hold values from -0.046875 to 0.046875
Outputs:
- grad_input: bfloat16 [3072, 4096], P(('dp', 'tensor'))
- grad_wgate: bfloat16 [4096, 14336], P('dp', 'tensor')
- grad_wup: bfloat16 [4096, 14336], P('dp', 'tensor')
- grad_wdown: bfloat16 [14336, 4096], P('tensor', 'dp')
The draws below stay inside these ranges and needn't reach their ends.
All inputs are finite; a program needn't handle non-finite values.
Results may differ from the reference program's by a relative error of at most 0.025.
Values may be sent and summed in bfloat16 or wider, within the bound.
No kernel may reach another device: no remote copies, remote signals or barrier semaphores. Data moves between devices by JAX's collectives and lax.ppermute only.
A program may use at most 128 MiB of HBM per device.

```python
import math
import jax
import jax.numpy as jnp
from jax import lax

D = 4096
FF = 14336
TOKENS = 3072
N_DP = 8


def strengthened(array, stream_key, source, target, shards_of, factor):
    def block_of(dim):
        return (jnp.arange(array.shape[dim]) // (array.shape[dim] // shards_of)).reshape((-1,) + (1,) * (array.ndim - 1 - dim))

    one_side = jax.random.permutation(stream_key, shards_of)[block_of(target)]
    far = (block_of(target) + shards_of // 2) % shards_of
    return jnp.where((block_of(source) == one_side) | (block_of(source) == far), factor * array, array)


def level_of(own_key, shape, cuts, low, high):
    def one(dim, shards_of):
        draws = jax.random.uniform(jax.random.fold_in(jax.random.fold_in(own_key, 6), dim), (shards_of,), jnp.float32, low / len(cuts), high / len(cuts))
        return jnp.repeat(jnp.exp(draws), shape[dim] // shards_of).reshape((-1,) + (1,) * (len(shape) - dim - 1))

    gain = one(*cuts[0])
    for cut in cuts[1:]:
        gain = gain * one(*cut)
    return gain


def bell_draw(own_key, dims, spread, most, pieces=(), kind=jnp.bfloat16):
    gain = level_of(own_key, dims, pieces, -0.22, 0.18) if pieces else 1.0
    array = jax.random.normal(own_key, dims, jnp.float32) * spread * gain
    return jnp.minimum(jnp.maximum(array, -most), most).astype(kind)


def bell_draw_with(rng, extent, spread, most, pieces, heavy, kind=jnp.bfloat16):
    array = spread * jax.random.normal(rng, extent, jnp.float32)
    if pieces:
        array = array * level_of(rng, extent, pieces, -0.22, 0.18)
    return jnp.clip(strengthened(array, jax.random.fold_in(rng, 3), *heavy), -most, most).astype(kind)


def setup_inputs(seed: int = 0) -> dict:
    seeds = jax.random.split(jax.random.key(seed), 7)
    x_stash = bell_draw(seeds[0], (TOKENS, D), 1.0, 4.0, ((0, 256),))
    x_scale = jnp.clip(jnp.exp(math.log(3.0) - 2.306499 * jax.random.uniform(seeds[1], (TOKENS,), jnp.float32) ** level_of(seeds[1], (TOKENS,), ((0, 256),), -0.2, 0.2)), 0.29882812, 3.0).astype(jnp.bfloat16)
    grad_out = bell_draw_with(seeds[2], (TOKENS, D), 0.25, 6.0, ((0, 256),), (0, 1, 256, 6.0))
    w_gate = bell_draw(seeds[3], (D, FF), D ** -0.5, 0.09375, ((1, 32),))
    w_up = bell_draw(seeds[4], (D, FF), D ** -0.5, 0.09375, ((1, 32),))
    w_down = bell_draw(seeds[5], (FF, D), FF ** -0.5, 0.046875, ((0, 32),))
    return dict(x_stash=x_stash, x_scale=x_scale, grad_out=grad_out, w_gate=w_gate, w_up=w_up, w_down=w_down)


def reference(x_stash, x_scale, grad_out, w_gate, w_up, w_down):
    inputs = (x_stash.astype(jnp.float32) * x_scale.astype(jnp.float32)[:, None]).astype(jnp.bfloat16)
    gate_value = jnp.dot(inputs, w_gate, preferred_element_type=jnp.float32)
    up_value = jnp.dot(inputs, w_up, preferred_element_type=jnp.float32)
    grad_hidden = lax.dot_general(grad_out, w_down, (((1,), (1,)), ((), ())), preferred_element_type=jnp.float32)
    logistic = jax.nn.sigmoid(gate_value)
    swish = gate_value * logistic
    hidden = (swish * up_value).astype(jnp.bfloat16)
    grad_up = (grad_hidden * swish).astype(jnp.bfloat16)
    grad_gate = (grad_hidden * up_value * logistic * (1.0 + gate_value * (1.0 - logistic))).astype(jnp.bfloat16)
    contract = (((1,), (1,)), ((), ()))
    grad_input = lax.dot_general(grad_gate, w_gate, contract, preferred_element_type=jnp.float32)
    grad_input = grad_input + lax.dot_general(grad_up, w_up, contract, preferred_element_type=jnp.float32)
    grad_input = grad_input.astype(jnp.bfloat16)
    group_rows = TOKENS // N_DP
    over_rows = (((0,), (0,)), ((), ()))

    def group_step(totals, group_index):
        begin = (group_index * group_rows).astype(jnp.int32)
        inp = lax.dynamic_slice_in_dim(inputs, begin, group_rows, 0)
        dgt = lax.dynamic_slice_in_dim(grad_gate, begin, group_rows, 0)
        dup = lax.dynamic_slice_in_dim(grad_up, begin, group_rows, 0)
        hid = lax.dynamic_slice_in_dim(hidden, begin, group_rows, 0)
        dyo = lax.dynamic_slice_in_dim(grad_out, begin, group_rows, 0)
        parts = (lax.dot_general(inp, dgt, over_rows, preferred_element_type=jnp.float32),
                 lax.dot_general(inp, dup, over_rows, preferred_element_type=jnp.float32),
                 lax.dot_general(hid, dyo, over_rows, preferred_element_type=jnp.float32))
        rounded = lax.optimization_barrier(tuple(p.astype(jnp.bfloat16) for p in parts))
        return tuple(t + r.astype(jnp.float32) for t, r in zip(totals, rounded)), None

    start_totals = (jnp.zeros((D, FF), jnp.float32), jnp.zeros((D, FF), jnp.float32), jnp.zeros((FF, D), jnp.float32))
    totals, unused = lax.scan(group_step, start_totals, jnp.arange(N_DP, dtype=jnp.int32))
    return (grad_input, totals[0].astype(jnp.bfloat16), totals[1].astype(jnp.bfloat16), totals[2].astype(jnp.bfloat16))
```

```python
import jax
import jax.numpy as jnp
from jax import lax
from jax.sharding import Mesh, PartitionSpec as P

BF = jnp.bfloat16
F32 = jnp.float32
SIZES = {"x": 4, "yh": 2, "z": 8, "yl": 2, "c": 2}
AXES = tuple(SIZES)


def shift(array, axis, by):
    n = SIZES[axis]
    return lax.ppermute(array, axis, [(i, (i + by) % n) for i in range(n)])


def ring_gather(block):
    half = block.shape[1] // 2
    back, ahead = [block], [block]
    for _ in range(3):
        back.append(shift(back[-1], "z", 1))
        ahead.append(shift(ahead[-1], "z", -1))
    far = jnp.concatenate(
        [shift(back[3][:, :half], "z", 1), shift(ahead[3][:, half:], "z", -1)], axis=1
    )
    return [block, back[1], ahead[1], back[2], ahead[2], back[3], ahead[3], far]


def ring_scatter(blocks):
    own, to_m1, to_p1, to_m2, to_p2, to_m3, to_p3, to_4 = blocks
    half = own.shape[1] // 2

    def add(a, b):
        return (a.astype(F32) + b.astype(F32)).astype(BF)

    right = shift(to_4[:, :half], "z", 1)
    left = shift(to_4[:, half:], "z", -1)
    right = jnp.concatenate([add(right, to_p3[:, :half]), to_p3[:, half:]], axis=1)
    left = jnp.concatenate([to_m3[:, :half], add(left, to_m3[:, half:])], axis=1)
    for right_term, left_term in ((to_p2, to_m2), (to_p1, to_m1)):
        right = add(shift(right, "z", 1), right_term)
        left = add(shift(left, "z", -1), left_term)
    right, left = shift(right, "z", 1), shift(left, "z", -1)
    return (right.astype(F32) + left.astype(F32) + own.astype(F32)).astype(BF)


def x_gather(array):
    half = array.shape[0] // 2
    before, after = shift(array, "x", 1), shift(array, "x", -1)
    far = jnp.concatenate(
        [shift(before[:half], "x", 1), shift(after[half:], "x", -1)], axis=0
    )
    return before, after, far


def dot(left, right, contract):
    return lax.dot_general(
        left, right, ((contract[:1], contract[1:]), ((), ())), preferred_element_type=F32
    )


def body(x_stash, x_scale, grad_out, w_gate, w_up, w_down):
    rows, width = x_stash.shape
    block = width // 4
    half_block = block // 2
    x, yh = lax.axis_index("x"), lax.axis_index("yh")
    gate_t, up_t = w_gate.T, w_up.T
    inputs = (x_stash.astype(F32) * x_scale.astype(F32)[:, None]).astype(BF)

    def columns(array, owner):
        first = lax.dynamic_slice_in_dim(array, owner * block + yh * half_block, half_block, 1)
        second = lax.dynamic_slice_in_dim(
            array, owner * block + (1 - yh) * half_block, half_block, 1
        )
        return jnp.concatenate([first, second], axis=1)

    pair = shift(jnp.concatenate([inputs, grad_out], axis=0), "yl", 1)
    in_block = jnp.concatenate([inputs, pair[:rows]], axis=0)
    go_block = jnp.concatenate([grad_out, pair[rows:]], axis=0)

    def both_cores(blocks):
        mine = jnp.concatenate(blocks, axis=0)
        return jnp.concatenate([mine, shift(mine, "c", 1)], axis=0)

    in_rows = both_cores(ring_gather(in_block))
    go_rows = both_cores(ring_gather(go_block))

    both = jnp.concatenate([in_block, go_block], axis=0)
    others = [shift(columns(both, (x + by) % 4), "x", by) for by in (1, 3, 2)]
    n = in_block.shape[0]
    others = ring_gather(jnp.concatenate(others, axis=0))
    others = jnp.stack(others)
    partner = shift(others, "c", 1)

    def cut(i):
        return jnp.concatenate(
            [a[:, i * n : (i + 1) * n].reshape(-1, block) for a in (others, partner)], axis=0
        )

    in_cols = jnp.concatenate([columns(in_rows, x), cut(0), cut(2), cut(4)], axis=0)
    go_cols = jnp.concatenate([columns(go_rows, x), cut(1), cut(3), cut(5)], axis=0)

    gate = dot(gate_t, in_rows, (1, 1))
    up = dot(up_t, in_rows, (1, 1))
    logistic = jax.nn.sigmoid(gate)
    swish = gate * logistic
    hidden = (swish * up).astype(BF)
    grad_hidden = dot(w_down, go_rows, (1, 1))
    grad_up = (grad_hidden * swish).astype(BF)
    grad_gate = (grad_hidden * up * logistic * (1.0 + gate * (1.0 - logistic))).astype(BF)

    def weight_grad(array, cols):
        full = jnp.concatenate([array, *x_gather(array)], axis=1)
        sent = shift(dot(full, cols[:, half_block:], (1, 0)).astype(BF), "yh", 1)
        own = dot(full, cols[:, :half_block], (1, 0))
        return (own + sent.astype(F32)).astype(BF)

    down = weight_grad(hidden, go_cols)
    up_grad = weight_grad(grad_up, in_cols)
    gate_grad = weight_grad(grad_gate, in_cols)

    terms = (dot(grad_gate, gate_t, (0, 0)) + dot(grad_up, up_t, (0, 0))).astype(BF)
    group = terms.shape[0] // 2
    terms = (terms[:group].astype(F32) + shift(terms[group:], "c", 1).astype(F32)).astype(BF)
    mine = ring_scatter([terms[i * n : (i + 1) * n] for i in range(8)])
    grad_input = (
        mine[:rows].astype(F32) + shift(mine[rows:], "yl", 1).astype(F32)
    ).astype(BF)
    return grad_input, gate_grad.T, up_grad.T, down


def solution(mesh):
    fine = Mesh(mesh.devices.reshape(tuple(SIZES.values())), AXES)
    dp, tensor = ("x", "yh"), ("z", "yl", "c")
    return jax.shard_map(
        body,
        mesh=fine,
        in_specs=(
            P(AXES, None),
            P(AXES),
            P(AXES, None),
            P(None, tensor),
            P(None, tensor),
            P(tensor, None),
        ),
        out_specs=(P(AXES, None), P(dp, tensor), P(dp, tensor), P(tensor, dp)),
        check_vma=False,
    )
```

```python
import functools

import jax
import jax.numpy as jnp
from jax import lax
from jax.experimental import pallas as pl
from jax.experimental.pallas import tpu as pltpu
from jax.sharding import Mesh, PartitionSpec as P

BF = jnp.bfloat16
F32 = jnp.float32
SIZES = {"x": 4, "yh": 2, "z": 8, "yl": 2, "c": 2}
AXES = tuple(SIZES)


def shift(array, axis, by):
    n = SIZES[axis]
    return lax.ppermute(array, axis, [(i, (i + by) % n) for i in range(n)])


def after(array, *others):
    return lax.optimization_barrier((array, *others))[0]


def together(*arrays):
    return lax.optimization_barrier(arrays)


def ring_step(state):
    back, ahead = state
    return shift(back, "z", 1), shift(ahead, "z", -1)


def ring_last(state):
    back, ahead = state
    half = back.shape[1] // 2
    return shift(back[:, :half], "z", 1), shift(ahead[:, half:], "z", -1)


def add(a, b):
    return (a.astype(F32) + b.astype(F32)).astype(BF)


def scatter_first(blocks):
    own, to_m1, to_p1, to_m2, to_p2, to_m3, to_p3, to_4 = blocks
    half = own.shape[1] // 2
    right = shift(to_4[:, :half], "z", 1)
    left = shift(to_4[:, half:], "z", -1)
    right = jnp.concatenate([add(right, to_p3[:, :half]), to_p3[:, half:]], axis=1)
    left = jnp.concatenate([to_m3[:, :half], add(left, to_m3[:, half:])], axis=1)
    return right, left


def scatter_step(sums, right_term, left_term):
    right, left = sums
    return add(shift(right, "z", 1), right_term), add(shift(left, "z", -1), left_term)


def scatter_last(sums, own):
    right, left = sums
    right, left = shift(right, "z", 1), shift(left, "z", -1)
    return (right.astype(F32) + left.astype(F32) + own.astype(F32)).astype(BF)


def x_first(array):
    return shift(array, "x", 1), shift(array, "x", -1)


def x_second(before, ahead):
    half = before.shape[0] // 2
    return shift(before[:half], "x", 1), shift(ahead[half:], "x", -1)


def copies(plan, inputs, shapes):
    def kernel(*refs):
        ins, outs, sems = refs[: len(inputs)], refs[len(inputs) : -1], refs[-1]
        pairs = plan(ins, outs)
        started = [pltpu.make_async_copy(a, b, sems.at[i]) for i, (a, b) in enumerate(pairs)]
        for one in started:
            one.start()
        for one in started:
            one.wait()

    moved = sum(2 * s[0] * s[1] * (s[2] if len(s) > 2 else 1) for s in shapes)
    return pl.pallas_call(
        kernel,
        out_shape=[jax.ShapeDtypeStruct(s, BF) for s in shapes],
        in_specs=[pl.BlockSpec(memory_space=pl.ANY)] * len(inputs),
        out_specs=[pl.BlockSpec(memory_space=pltpu.VMEM)] * len(shapes),
        scratch_shapes=[pltpu.SemaphoreType.DMA((48 + 6,))],
        compiler_params=pltpu.CompilerParams(vmem_limit_bytes=16 * 2**20),
        cost_estimate=pl.CostEstimate(flops=0, bytes_accessed=2 * moved, transcendentals=0),
    )(*inputs)


def stack_rows(pieces, first, rows):
    width = pieces[0].shape[1]

    def plan(ins, outs):
        cut = pl.ds(first, rows)
        pairs = [(ins[i].at[cut], outs[0].at[pl.ds(rows * i, rows)]) for i in range(7)]
        for i in range(2):
            view = outs[0].at[pl.ds(rows * 7, rows), pl.ds(i * (width // 2), width // 2)]
            pairs.append((ins[7 + i].at[cut], view))
        return pairs

    return copies(plan, pieces, [(8 * rows, width)])[0]


def stack_sources(pieces, rows):
    total, width = pieces[0].shape
    n = total // rows

    def plan(ins, outs):
        pairs = []
        for s in range(n):
            cut = pl.ds(s * rows, rows)
            for i in range(7):
                pairs.append((ins[i].at[cut], outs[0].at[s, pl.ds(rows * i, rows)]))
            for i in range(2):
                view = outs[0].at[s, pl.ds(rows * 7, rows), pl.ds(i * (width // 2), width // 2)]
                pairs.append((ins[7 + i].at[cut], view))
        return pairs

    return copies(plan, pieces, [(n, 8 * rows, width)])[0]


def merge_halves(own, other, c_of):
    rows, half = own.shape
    part = half // 4

    def plan(ins, outs):
        c = lax.axis_index("c")
        pairs = []
        for j in range(4):
            for ref, k in ((ins[0], c), (ins[1], 1 - c)):
                at = pl.multiple_of(j * 2 * part + k * part, part)
                pairs.append((ref.at[:, pl.ds(j * part, part)], outs[0].at[:, pl.ds(at, part)]))
        return pairs

    return copies(plan, [own, other], [(rows, 2 * half)])[0]


def split_halves(array):
    rows, width = array.shape
    part = width // 8

    def plan(ins, outs):
        c = lax.axis_index("c")
        pairs = []
        for j in range(4):
            for i, k in ((0, c), (1, 1 - c)):
                at = pl.multiple_of(j * 2 * part + k * part, part)
                pairs.append((ins[0].at[:, pl.ds(at, part)], outs[i].at[:, pl.ds(j * part, part)]))
        return pairs

    return copies(plan, [array], [(rows, width // 2)] * 2)


def dot(left, right, contract):
    return lax.dot_general(
        left, right, ((contract[:1], contract[1:]), ((), ())), preferred_element_type=F32
    )


def body(x_stash, x_scale, grad_out, w_gate, w_up, w_down):
    rows, width = x_stash.shape
    quarter = width // 8
    x, yh, c = lax.axis_index("x"), lax.axis_index("yh"), lax.axis_index("c")
    gate_t, up_t = w_gate.T, w_up.T
    inputs = (x_stash.astype(F32) * x_scale.astype(F32)[:, None]).astype(BF)

    def core_columns(array, core):
        at = [j * 2 * quarter + core * quarter for j in range(4)]
        return jnp.concatenate(
            [lax.dynamic_slice_in_dim(array, a, quarter, 1) for a in at], axis=1
        )

    pair = jnp.concatenate([inputs, grad_out], axis=0)
    mine, others = core_columns(pair, c), core_columns(pair, 1 - c)
    core = shift(others, "c", 1)
    along = shift(mine, "yl", 1)
    across = lax.ppermute(others, ("yl", "c"), [(0, 3), (1, 2), (2, 1), (3, 0)])
    ordered = [
        jnp.where(c == 0, mine, core),
        jnp.where(c == 0, core, mine),
        jnp.where(c == 0, along, across),
        jnp.where(c == 0, across, along),
    ]
    in_block = jnp.concatenate([a[:rows] for a in ordered], axis=0)
    go_block = jnp.concatenate([a[rows:] for a in ordered], axis=0)
    n = in_block.shape[0]

    both = jnp.concatenate([in_block, go_block], axis=0)
    far = [lax.dynamic_slice_in_dim(both, (x + by) % 4 * quarter, quarter, 1) for by in (1, 3, 2)]
    far = [shift(a, "x", by) for a, by in zip(far, (1, 3, 2))]

    state = (both, both)
    ring = [both]
    for step in range(3):
        state = ring_step(state)
        if step == 0:
            state, far = lax.optimization_barrier((state, far))
        ring += state
    last = ring_last(state)
    ring += last
    in_own = stack_rows(ring, 0, n)
    in_other = shift(in_own, "c", 1)
    go_own = stack_rows(ring, n, n)
    go_other = shift(go_own, "c", 1)
    far_block = after(jnp.concatenate(far, axis=0), last)
    far_1 = ring_step((far_block, far_block))
    in_rows = merge_halves(in_own, in_other, c)
    gate = dot(gate_t, in_rows, (1, 1))
    up = dot(up_t, in_rows, (1, 1))
    logistic = jax.nn.sigmoid(gate)
    swish = gate * logistic
    hidden = (swish * up).astype(BF)
    gate, up, hidden, go_own, go_other, far_1 = together(
        gate, up, hidden, go_own, go_other, far_1
    )
    far_2 = ring_step(far_1)
    go_rows = merge_halves(go_own, go_other, c)
    grad_hidden = dot(w_down, go_rows, (1, 1))
    logistic = jax.nn.sigmoid(gate)
    swish = gate * logistic
    grad_up = (grad_hidden * swish).astype(BF)
    grad_gate = (grad_hidden * up * logistic * (1.0 + gate * (1.0 - logistic))).astype(BF)
    both = jnp.concatenate([grad_up, grad_gate], axis=0)
    both, grad_up, grad_gate, far_2, hidden = together(both, grad_up, grad_gate, far_2, hidden)

    both_1 = x_first(both)
    far_3 = ring_step(far_2)
    terms = (dot(grad_gate, gate_t, (0, 0)) + dot(grad_up, up_t, (0, 0))).astype(BF)
    mine, others = split_halves(terms)
    both, both_1, far_3, mine, others, hidden = together(
        both, both_1, far_3, mine, others, hidden
    )

    both_2 = x_second(*both_1)
    far_4 = ring_last(far_3)
    got = shift(others, "c", 1)
    both_2, far_4, mine, got, hidden = together(both_2, far_4, mine, got, hidden)
    hidden_1 = x_first(hidden)
    far_own = stack_sources([far_block, *far_1, *far_2, *far_3, *far_4], n)
    far_other = shift(far_own, "c", 1)
    terms = add(mine, got)
    hidden_1, terms, far_own, far_other = together(hidden_1, terms, far_own, far_other)

    def columns(rows_own, far, i):
        own = lax.dynamic_slice_in_dim(rows_own, x * quarter, quarter, 1)
        return jnp.concatenate([own, far[i], far[2 + i], far[4 + i]], axis=0)

    def weight_terms(array, near, far, i, own, other):
        full = jnp.concatenate([array, *near, jnp.concatenate(far, axis=0)], axis=1)
        first = dot(full, columns(own, far_own, i), (1, 0)).astype(BF)
        second = dot(full, columns(other, far_other, i), (1, 0)).astype(BF)
        return jnp.where(c == yh, first, second), jnp.where(c == yh, second, first)

    ff = hidden.shape[0]
    blocks = [terms[i * n : (i + 1) * n] for i in range(8)]
    hidden_2 = x_second(*hidden_1)
    sums = scatter_first(blocks)
    kept, sent = weight_terms(both, both_1, both_2, 0, in_own, in_other)
    got = shift(sent, "yh", 1)
    sums, hidden_2, sent = together(sums, hidden_2, sent)
    sums = scatter_step(sums, blocks[4], blocks[3])
    down_kept, down_sent = weight_terms(hidden, hidden_1, hidden_2, 1, go_own, go_other)
    down_got = shift(down_sent, "yh", 1)
    sums, down_sent = together(sums, down_sent)
    sums = scatter_step(sums, blocks[2], blocks[1])
    sums, got = together(sums, got)
    block = scatter_last(sums, blocks[0])
    up_grad, gate_grad = add(kept[:ff], got[:ff]), add(kept[ff:], got[ff:])
    block, down_got = together(block, down_got)
    down = add(down_kept, down_got)
    half = n // 2
    block = block[:half].astype(F32) + shift(block[half:], "yl", 1).astype(F32)
    block = block.astype(BF)
    first, second = block[:rows], block[rows:]
    keep = jnp.where(c == 0, first, second)
    got = shift(jnp.where(c == 0, second, first), "c", 1)
    low, high = jnp.where(c == 0, keep, got), jnp.where(c == 0, got, keep)
    parts = []
    for j in range(4):
        cut = slice(j * quarter, (j + 1) * quarter)
        parts += [low[:, cut], high[:, cut]]
    return jnp.concatenate(parts, axis=1), gate_grad.T, up_grad.T, down


def solution(mesh):
    fine = Mesh(mesh.devices.reshape(tuple(SIZES.values())), AXES)
    dp, tensor = ("x", "yh"), ("z", "yl", "c")
    return jax.shard_map(
        body,
        mesh=fine,
        in_specs=(
            P(AXES, None),
            P(AXES),
            P(AXES, None),
            P(None, tensor),
            P(None, tensor),
            P(tensor, None),
        ),
        out_specs=(P(AXES, None), P(dp, tensor), P(dp, tensor), P(tensor, dp)),
        check_vma=False,
    )
```

```python
import functools

import jax
import jax.numpy as jnp
from jax import lax
from jax.experimental import pallas as pl
from jax.experimental.pallas import tpu as pltpu
from jax.sharding import Mesh, PartitionSpec as P

BF = jnp.bfloat16
F32 = jnp.float32
SIZES = {"x": 4, "yh": 2, "z": 8, "yl": 2, "c": 2}
AXES = tuple(SIZES)


def shift(array, axis, by):
    n = SIZES[axis]
    return lax.ppermute(array, axis, [(i, (i + by) % n) for i in range(n)])


def after(array, *others):
    return lax.optimization_barrier((array, *others))[0]


def together(*arrays):
    return lax.optimization_barrier(arrays)


def ring_step(state):
    back, ahead = state
    return shift(back, "z", 1), shift(ahead, "z", -1)


def ring_last(state):
    back, ahead = state
    half = back.shape[1] // 2
    return shift(back[:, :half], "z", 1), shift(ahead[:, half:], "z", -1)


def add(a, b):
    return (a.astype(F32) + b.astype(F32)).astype(BF)


def scatter_first(blocks):
    own, to_m1, to_p1, to_m2, to_p2, to_m3, to_p3, to_4 = blocks
    half = own.shape[1] // 2
    right = shift(to_4[:, :half], "z", 1)
    left = shift(to_4[:, half:], "z", -1)
    right = jnp.concatenate([add(right, to_p3[:, :half]), to_p3[:, half:]], axis=1)
    left = jnp.concatenate([to_m3[:, :half], add(left, to_m3[:, half:])], axis=1)
    return right, left


def scatter_step(sums, right_term, left_term):
    right, left = sums
    return add(shift(right, "z", 1), right_term), add(shift(left, "z", -1), left_term)


def scatter_last(sums, own):
    right, left = sums
    right, left = shift(right, "z", 1), shift(left, "z", -1)
    return (right.astype(F32) + left.astype(F32) + own.astype(F32)).astype(BF)


def x_first(array):
    return shift(array, "x", 1), shift(array, "x", -1)


def x_second(before, ahead):
    half = before.shape[0] // 2
    return shift(before[:half], "x", 1), shift(ahead[half:], "x", -1)


def copies(plan, inputs, shapes):
    def kernel(*refs):
        ins, outs, sems = refs[: len(inputs)], refs[len(inputs) : -1], refs[-1]
        pairs, chosen = plan(ins, outs)
        started = [pltpu.make_async_copy(a, b, sems.at[i]) for i, (a, b) in enumerate(pairs)]
        for one in started:
            one.start()
        for i, (when, a, b) in enumerate(chosen):

            @pl.when(when)
            def one_of():
                one = pltpu.make_async_copy(a, b, sems.at[len(pairs) + i])
                one.start()
                one.wait()

        for one in started:
            one.wait()

    return pl.pallas_call(
        kernel,
        out_shape=[jax.ShapeDtypeStruct(s, BF) for s in shapes],
        in_specs=[pl.BlockSpec(memory_space=pl.ANY)] * len(inputs),
        out_specs=[pl.BlockSpec(memory_space=pltpu.VMEM)] * len(shapes),
        scratch_shapes=[pltpu.SemaphoreType.DMA((54,))],
        compiler_params=pltpu.CompilerParams(vmem_limit_bytes=16 * 2**20),
        cost_estimate=pl.CostEstimate(flops=0, bytes_accessed=0, transcendentals=0),
    )(*inputs)


def x_columns(width):
    return pl.ds(pl.multiple_of(lax.axis_index("x") * width, width), width)


def stack_rows(pieces, first, rows):
    width = pieces[0].shape[1]
    part = width // 4

    def plan(ins, outs):
        cut = pl.ds(first, rows)
        pairs = [(ins[i].at[cut], outs[0].at[pl.ds(rows * i, rows)]) for i in range(7)]
        for i in range(2):
            view = outs[0].at[pl.ds(rows * 7, rows), pl.ds(i * (width // 2), width // 2)]
            pairs.append((ins[7 + i].at[cut], view))
        x = lax.axis_index("x")
        own = x_columns(part)
        pairs += [(ins[i].at[cut, own], outs[1].at[pl.ds(rows * i, rows)]) for i in range(7)]
        at = pl.multiple_of(x % 2 * part, part)
        last = outs[1].at[pl.ds(rows * 7, rows)]
        return pairs, [(x // 2 == i, ins[7 + i].at[cut, pl.ds(at, part)], last) for i in range(2)]

    return copies(plan, pieces, [(8 * rows, width), (8 * rows, part)])


def stack_sources(pieces, rows):
    total, width = pieces[0].shape
    n = total // rows

    def plan(ins, outs):
        pairs = []
        for s in range(n):
            cut = pl.ds(s * rows, rows)
            for i in range(7):
                pairs.append((ins[i].at[cut], outs[0].at[s, pl.ds(rows * i, rows)]))
            for i in range(2):
                view = outs[0].at[s, pl.ds(rows * 7, rows), pl.ds(i * (width // 2), width // 2)]
                pairs.append((ins[7 + i].at[cut], view))
        return pairs, []

    return copies(plan, pieces, [(n, 8 * rows, width)])[0]


def merge_halves(own, other):
    rows, half = own.shape
    part = half // 4

    def plan(ins, outs):
        c = lax.axis_index("c")
        pairs = []
        for j in range(4):
            for ref, k in ((ins[0], c), (ins[1], 1 - c)):
                at = pl.multiple_of(j * 2 * part + k * part, part)
                pairs.append((ref.at[:, pl.ds(j * part, part)], outs[0].at[:, pl.ds(at, part)]))
        pairs.append((ins[1].at[:, x_columns(part)], outs[1]))
        return pairs, []

    return copies(plan, [own, other], [(rows, 2 * half), (rows, part)])


def split_halves(array):
    rows, width = array.shape
    part = width // 8

    def plan(ins, outs):
        c = lax.axis_index("c")
        pairs = []
        for j in range(4):
            for i, k in ((0, c), (1, 1 - c)):
                at = pl.multiple_of(j * 2 * part + k * part, part)
                pairs.append((ins[0].at[:, pl.ds(at, part)], outs[i].at[:, pl.ds(j * part, part)]))
        return pairs, []

    return copies(plan, [array], [(rows, width // 2)] * 2)


def dot(left, right, contract):
    return lax.dot_general(
        left, right, ((contract[:1], contract[1:]), ((), ())), preferred_element_type=F32
    )


def body(x_stash, x_scale, grad_out, w_gate, w_up, w_down):
    rows, width = x_stash.shape
    quarter = width // 8
    x, yh, c = lax.axis_index("x"), lax.axis_index("yh"), lax.axis_index("c")
    gate_t, up_t = w_gate.T, w_up.T
    inputs = (x_stash.astype(F32) * x_scale.astype(F32)[:, None]).astype(BF)

    def core_columns(array, core):
        at = [j * 2 * quarter + core * quarter for j in range(4)]
        return jnp.concatenate(
            [lax.dynamic_slice_in_dim(array, a, quarter, 1) for a in at], axis=1
        )

    pair = jnp.concatenate([inputs, grad_out], axis=0)
    mine, others = core_columns(pair, c), core_columns(pair, 1 - c)
    core = shift(others, "c", 1)
    along = shift(mine, "yl", 1)
    across = lax.ppermute(others, ("yl", "c"), [(0, 3), (1, 2), (2, 1), (3, 0)])
    ordered = [
        jnp.where(c == 0, mine, core),
        jnp.where(c == 0, core, mine),
        jnp.where(c == 0, along, across),
        jnp.where(c == 0, across, along),
    ]
    in_block = jnp.concatenate([a[:rows] for a in ordered], axis=0)
    go_block = jnp.concatenate([a[rows:] for a in ordered], axis=0)
    n = in_block.shape[0]

    both = jnp.concatenate([in_block, go_block], axis=0)
    far = [lax.dynamic_slice_in_dim(both, (x + by) % 4 * quarter, quarter, 1) for by in (1, 3, 2)]
    far = [shift(a, "x", by) for a, by in zip(far, (1, 3, 2))]

    state = (both, both)
    ring = [both]
    for step in range(3):
        state = ring_step(state)
        if step == 0:
            state, far = lax.optimization_barrier((state, far))
        ring += state
    far_block = jnp.concatenate(far, axis=0)
    last, far_1 = together(ring_last(state), ring_step((far_block, far_block)))
    ring += last
    in_own, in_cols = stack_rows(ring, 0, n)
    in_other = shift(in_own, "c", 1)
    go_own, go_cols = stack_rows(ring, n, n)
    go_other = shift(go_own, "c", 1)
    far_2 = ring_step(far_1)
    in_rows, in_cols_other = merge_halves(in_own, in_other)
    gate = dot(gate_t, in_rows, (1, 1))
    up = dot(up_t, in_rows, (1, 1))
    logistic = jax.nn.sigmoid(gate)
    swish = gate * logistic
    hidden = (swish * up).astype(BF)
    gate, up, hidden, go_own, go_other, far_2 = together(
        gate, up, hidden, go_own, go_other, far_2
    )
    far_3 = ring_step(far_2)
    go_rows, go_cols_other = merge_halves(go_own, go_other)
    grad_hidden = dot(w_down, go_rows, (1, 1))
    logistic = jax.nn.sigmoid(gate)
    swish = gate * logistic
    grad_up = (grad_hidden * swish).astype(BF)
    grad_gate = (grad_hidden * up * logistic * (1.0 + gate * (1.0 - logistic))).astype(BF)
    both = jnp.concatenate([grad_up, grad_gate], axis=0)
    both, grad_up, grad_gate, far_3, hidden = together(both, grad_up, grad_gate, far_3, hidden)

    both_1 = x_first(both)
    far_4 = ring_last(far_3)
    terms = (dot(grad_gate, gate_t, (0, 0)) + dot(grad_up, up_t, (0, 0))).astype(BF)
    mine, others = split_halves(terms)
    far_own = stack_sources([far_block, *far_1, *far_2, *far_3, *far_4], n)
    both, both_1, mine, others, far_own, hidden = together(
        both, both_1, mine, others, far_own, hidden
    )

    both_2 = x_second(*both_1)
    hidden_1 = x_first(hidden)
    far_other = shift(far_own, "c", 1)
    terms = add(mine, shift(others, "c", 1))
    blocks = [terms[i * n : (i + 1) * n] for i in range(8)]
    sums = scatter_first(blocks)
    both_2, hidden_1, far_other, sums = together(both_2, hidden_1, far_other, sums)

    def columns(own, far, i):
        return jnp.concatenate([own, far[i], far[2 + i], far[4 + i]], axis=0)

    def weight_terms(array, near, far, i, own, other):
        full = jnp.concatenate([array, *near, jnp.concatenate(far, axis=0)], axis=1)
        first = dot(full, columns(own, far_own, i), (1, 0)).astype(BF)
        second = dot(full, columns(other, far_other, i), (1, 0)).astype(BF)
        return jnp.where(c == yh, first, second), jnp.where(c == yh, second, first)

    ff = hidden.shape[0]
    hidden_2 = x_second(*hidden_1)
    sums = scatter_step(sums, blocks[4], blocks[3])
    kept, sent = weight_terms(both, both_1, both_2, 0, in_cols, in_cols_other)
    got = shift(sent, "yh", 1)
    sums, hidden_2, sent = together(sums, hidden_2, sent)
    sums = scatter_step(sums, blocks[2], blocks[1])
    down_kept, down_sent = weight_terms(hidden, hidden_1, hidden_2, 1, go_cols, go_cols_other)
    down_got = shift(down_sent, "yh", 1)
    sums, down_sent = together(sums, down_sent)
    block = scatter_last(sums, blocks[0])
    block, got = together(block, got)
    up_grad, gate_grad = add(kept[:ff], got[:ff]), add(kept[ff:], got[ff:])
    half = n // 2
    block = block[:half].astype(F32) + shift(block[half:], "yl", 1).astype(F32)
    block = block.astype(BF)
    block, down_got = together(block, down_got)
    down = add(down_kept, down_got)
    first, second = block[:rows], block[rows:]
    keep = jnp.where(c == 0, first, second)
    got = shift(jnp.where(c == 0, second, first), "c", 1)
    low, high = jnp.where(c == 0, keep, got), jnp.where(c == 0, got, keep)
    parts = []
    for j in range(4):
        cut = slice(j * quarter, (j + 1) * quarter)
        parts += [low[:, cut], high[:, cut]]
    return jnp.concatenate(parts, axis=1), gate_grad.T, up_grad.T, down


def solution(mesh):
    fine = Mesh(mesh.devices.reshape(tuple(SIZES.values())), AXES)
    dp, tensor = ("x", "yh"), ("z", "yl", "c")
    return jax.shard_map(
        body,
        mesh=fine,
        in_specs=(
            P(AXES, None),
            P(AXES),
            P(AXES, None),
            P(None, tensor),
            P(None, tensor),
            P(tensor, None),
        ),
        out_specs=(P(AXES, None), P(dp, tensor), P(dp, tensor), P(tensor, dp)),
        check_vma=False,
    )
```

```python
import functools

import jax
import jax.numpy as jnp
from jax import lax
from jax.experimental import pallas as pl
from jax.experimental.pallas import tpu as pltpu
from jax.sharding import Mesh, PartitionSpec as P

BF = jnp.bfloat16
F32 = jnp.float32
SIZES = {"x": 4, "yh": 2, "z": 8, "yl": 2, "c": 2}
AXES = tuple(SIZES)


def shift(array, axis, by):
    n = SIZES[axis]
    return lax.ppermute(array, axis, [(i, (i + by) % n) for i in range(n)])


def after(array, *others):
    return lax.optimization_barrier((array, *others))[0]


def together(*arrays):
    return lax.optimization_barrier(arrays)


def ring_step(state):
    back, ahead = state
    return shift(back, "z", 1), shift(ahead, "z", -1)


def ring_last(state):
    back, ahead = state
    half = back.shape[1] // 2
    return shift(back[:, :half], "z", 1), shift(ahead[:, half:], "z", -1)


def add(a, b):
    return (a.astype(F32) + b.astype(F32)).astype(BF)


def scatter_first(blocks):
    own, to_m1, to_p1, to_m2, to_p2, to_m3, to_p3, to_4 = blocks
    half = own.shape[1] // 2
    right = shift(to_4[:, :half], "z", 1)
    left = shift(to_4[:, half:], "z", -1)
    right = jnp.concatenate([add(right, to_p3[:, :half]), to_p3[:, half:]], axis=1)
    left = jnp.concatenate([to_m3[:, :half], add(left, to_m3[:, half:])], axis=1)
    return right, left


def scatter_step(sums, right_term, left_term):
    right, left = sums
    return add(shift(right, "z", 1), right_term), add(shift(left, "z", -1), left_term)


def scatter_last(sums, own):
    right, left = sums
    right, left = shift(right, "z", 1), shift(left, "z", -1)
    return (right.astype(F32) + left.astype(F32) + own.astype(F32)).astype(BF)


def x_first(array):
    return shift(array, "x", 1), shift(array, "x", -1)


def x_second(before, ahead):
    half = before.shape[0] // 2
    return shift(before[:half], "x", 1), shift(ahead[half:], "x", -1)


def copies(plan, inputs, shapes):
    def kernel(*refs):
        pairs, chosen = plan(refs[: len(inputs)], refs[len(inputs) :])
        for a, b in pairs:
            b[...] = a[...]
        for when, a, b in chosen:

            @pl.when(when)
            def one_of():
                b[...] = a[...]

    return pl.pallas_call(
        kernel,
        out_shape=[jax.ShapeDtypeStruct(s, BF) for s in shapes],
        in_specs=[pl.BlockSpec(memory_space=pltpu.VMEM)] * len(inputs),
        out_specs=[pl.BlockSpec(memory_space=pltpu.VMEM)] * len(shapes),
        compiler_params=pltpu.CompilerParams(vmem_limit_bytes=24 * 2**20),
        cost_estimate=pl.CostEstimate(flops=0, bytes_accessed=0, transcendentals=0),
    )(*inputs)


def x_columns(width):
    return pl.ds(pl.multiple_of(lax.axis_index("x") * width, width), width)


def stack_rows(pieces, first, rows):
    width = pieces[0].shape[1]
    part = width // 4

    def plan(ins, outs):
        cut = pl.ds(first, rows)
        pairs = [(ins[i].at[cut], outs[0].at[pl.ds(rows * i, rows)]) for i in range(7)]
        for i in range(2):
            view = outs[0].at[pl.ds(rows * 7, rows), pl.ds(i * (width // 2), width // 2)]
            pairs.append((ins[7 + i].at[cut], view))
        x = lax.axis_index("x")
        own = x_columns(part)
        pairs += [(ins[i].at[cut, own], outs[1].at[pl.ds(rows * i, rows)]) for i in range(7)]
        at = pl.multiple_of(x % 2 * part, part)
        last = outs[1].at[pl.ds(rows * 7, rows)]
        return pairs, [(x // 2 == i, ins[7 + i].at[cut, pl.ds(at, part)], last) for i in range(2)]

    return copies(plan, pieces, [(8 * rows, width), (8 * rows, part)])


def stack_sources(pieces, rows):
    total, width = pieces[0].shape
    n = total // rows

    def plan(ins, outs):
        pairs = []
        for s in range(n):
            cut = pl.ds(s * rows, rows)
            for i in range(7):
                pairs.append((ins[i].at[cut], outs[0].at[s, pl.ds(rows * i, rows)]))
            for i in range(2):
                view = outs[0].at[s, pl.ds(rows * 7, rows), pl.ds(i * (width // 2), width // 2)]
                pairs.append((ins[7 + i].at[cut], view))
        return pairs, []

    return copies(plan, pieces, [(n, 8 * rows, width)])[0]


def merge_halves(own, other):
    rows, half = own.shape
    part = half // 4

    def plan(ins, outs):
        c = lax.axis_index("c")
        pairs = []
        for j in range(4):
            for ref, k in ((ins[0], c), (ins[1], 1 - c)):
                at = pl.multiple_of(j * 2 * part + k * part, part)
                pairs.append((ref.at[:, pl.ds(j * part, part)], outs[0].at[:, pl.ds(at, part)]))
        pairs.append((ins[1].at[:, x_columns(part)], outs[1]))
        return pairs, []

    return copies(plan, [own, other], [(rows, 2 * half), (rows, part)])


def split_halves(array):
    rows, width = array.shape
    part = width // 8

    def plan(ins, outs):
        c = lax.axis_index("c")
        pairs = []
        for j in range(4):
            for i, k in ((0, c), (1, 1 - c)):
                at = pl.multiple_of(j * 2 * part + k * part, part)
                pairs.append((ins[0].at[:, pl.ds(at, part)], outs[i].at[:, pl.ds(j * part, part)]))
        return pairs, []

    return copies(plan, [array], [(rows, width // 2)] * 2)


def dot(left, right, contract):
    return lax.dot_general(
        left, right, ((contract[:1], contract[1:]), ((), ())), preferred_element_type=F32
    )


def body(x_stash, x_scale, grad_out, w_gate, w_up, w_down):
    rows, width = x_stash.shape
    quarter = width // 8
    x, yh, c = lax.axis_index("x"), lax.axis_index("yh"), lax.axis_index("c")
    gate_t, up_t = w_gate.T, w_up.T
    inputs = (x_stash.astype(F32) * x_scale.astype(F32)[:, None]).astype(BF)

    def core_columns(array, core):
        at = [j * 2 * quarter + core * quarter for j in range(4)]
        return jnp.concatenate(
            [lax.dynamic_slice_in_dim(array, a, quarter, 1) for a in at], axis=1
        )

    pair = jnp.concatenate([inputs, grad_out], axis=0)
    mine, others = core_columns(pair, c), core_columns(pair, 1 - c)
    core = shift(others, "c", 1)
    along = shift(mine, "yl", 1)
    across = lax.ppermute(others, ("yl", "c"), [(0, 3), (1, 2), (2, 1), (3, 0)])
    ordered = [
        jnp.where(c == 0, mine, core),
        jnp.where(c == 0, core, mine),
        jnp.where(c == 0, along, across),
        jnp.where(c == 0, across, along),
    ]
    in_block = jnp.concatenate([a[:rows] for a in ordered], axis=0)
    go_block = jnp.concatenate([a[rows:] for a in ordered], axis=0)
    n = in_block.shape[0]

    both = jnp.concatenate([in_block, go_block], axis=0)
    far = [lax.dynamic_slice_in_dim(both, (x + by) % 4 * quarter, quarter, 1) for by in (1, 3, 2)]
    far = [shift(a, "x", by) for a, by in zip(far, (1, 3, 2))]

    state = (both, both)
    ring = [both]
    for step in range(3):
        state = ring_step(state)
        if step == 0:
            state, far = lax.optimization_barrier((state, far))
        ring += state
    far_block = jnp.concatenate(far, axis=0)
    last, far_1 = together(ring_last(state), ring_step((far_block, far_block)))
    ring += last
    in_own, in_cols = stack_rows(ring, 0, n)
    in_other = shift(in_own, "c", 1)
    go_own, go_cols = stack_rows(ring, n, n)
    go_other = shift(go_own, "c", 1)
    far_2 = ring_step(far_1)
    in_rows, in_cols_other = merge_halves(in_own, in_other)
    gate = dot(gate_t, in_rows, (1, 1))
    up = dot(up_t, in_rows, (1, 1))
    logistic = jax.nn.sigmoid(gate)
    swish = gate * logistic
    hidden = (swish * up).astype(BF)
    gate, up, hidden, go_own, go_other, far_2 = together(
        gate, up, hidden, go_own, go_other, far_2
    )
    far_3 = ring_step(far_2)
    go_rows, go_cols_other = merge_halves(go_own, go_other)
    grad_hidden = dot(w_down, go_rows, (1, 1))
    logistic = jax.nn.sigmoid(gate)
    swish = gate * logistic
    grad_up = (grad_hidden * swish).astype(BF)
    grad_gate = (grad_hidden * up * logistic * (1.0 + gate * (1.0 - logistic))).astype(BF)
    both = jnp.concatenate([grad_up, grad_gate], axis=0)
    both, grad_up, grad_gate, far_3, hidden = together(both, grad_up, grad_gate, far_3, hidden)

    both_1 = x_first(both)
    far_4 = ring_last(far_3)
    terms = (dot(grad_gate, gate_t, (0, 0)) + dot(grad_up, up_t, (0, 0))).astype(BF)
    mine, others = split_halves(terms)
    far_own = stack_sources([far_block, *far_1, *far_2, *far_3, *far_4], n)
    both, both_1, mine, others, far_own, hidden = together(
        both, both_1, mine, others, far_own, hidden
    )

    both_2 = x_second(*both_1)
    hidden_1 = x_first(hidden)
    far_other = shift(far_own, "c", 1)
    terms = add(mine, shift(others, "c", 1))
    blocks = [terms[i * n : (i + 1) * n] for i in range(8)]
    sums = scatter_first(blocks)
    both_2, hidden_1, far_other, sums = together(both_2, hidden_1, far_other, sums)

    def columns(own, far, i):
        return jnp.concatenate([own, far[i], far[2 + i], far[4 + i]], axis=0)

    def weight_terms(array, near, far, i, own, other):
        full = jnp.concatenate([array, *near, jnp.concatenate(far, axis=0)], axis=1)
        first = dot(full, columns(own, far_own, i), (1, 0)).astype(BF)
        second = dot(full, columns(other, far_other, i), (1, 0)).astype(BF)
        return jnp.where(c == yh, first, second), jnp.where(c == yh, second, first)

    ff = hidden.shape[0]
    hidden_2 = x_second(*hidden_1)
    sums = scatter_step(sums, blocks[4], blocks[3])
    kept, sent = weight_terms(both, both_1, both_2, 0, in_cols, in_cols_other)
    got = shift(sent, "yh", 1)
    sums, hidden_2, sent = together(sums, hidden_2, sent)
    sums = scatter_step(sums, blocks[2], blocks[1])
    down_kept, down_sent = weight_terms(hidden, hidden_1, hidden_2, 1, go_cols, go_cols_other)
    down_got = shift(down_sent, "yh", 1)
    sums, down_sent = together(sums, down_sent)
    block = scatter_last(sums, blocks[0])
    block, got = together(block, got)
    up_grad, gate_grad = add(kept[:ff], got[:ff]), add(kept[ff:], got[ff:])
    half = n // 2
    block = block[:half].astype(F32) + shift(block[half:], "yl", 1).astype(F32)
    block = block.astype(BF)
    first, second = block[:rows], block[rows:]
    keep = jnp.where(c == 0, first, second)
    got = shift(jnp.where(c == 0, second, first), "c", 1)
    got, down_got = together(got, down_got)
    down = add(down_kept, down_got)
    low, high = jnp.where(c == 0, keep, got), jnp.where(c == 0, got, keep)
    parts = []
    for j in range(4):
        cut = slice(j * quarter, (j + 1) * quarter)
        parts += [low[:, cut], high[:, cut]]
    return jnp.concatenate(parts, axis=1), gate_grad.T, up_grad.T, down


def solution(mesh):
    fine = Mesh(mesh.devices.reshape(tuple(SIZES.values())), AXES)
    dp, tensor = ("x", "yh"), ("z", "yl", "c")
    return jax.shard_map(
        body,
        mesh=fine,
        in_specs=(
            P(AXES, None),
            P(AXES),
            P(AXES, None),
            P(None, tensor),
            P(None, tensor),
            P(tensor, None),
        ),
        out_specs=(P(AXES, None), P(dp, tensor), P(dp, tensor), P(tensor, dp)),
        check_vma=False,
    )
```

```python
import functools

import jax
import jax.numpy as jnp
from jax import lax
from jax.experimental import pallas as pl
from jax.experimental.pallas import tpu as pltpu
from jax.sharding import Mesh, PartitionSpec as P

BF = jnp.bfloat16
F32 = jnp.float32
SIZES = {"x": 4, "yh": 2, "z": 8, "yl": 2, "c": 2}
AXES = tuple(SIZES)


def shift(array, axis, by):
    n = SIZES[axis]
    return lax.ppermute(array, axis, [(i, (i + by) % n) for i in range(n)])


def after(array, *others):
    return lax.optimization_barrier((array, *others))[0]


def together(*arrays):
    return lax.optimization_barrier(arrays)


def ring_step(state):
    back, ahead = state
    return shift(back, "z", 1), shift(ahead, "z", -1)


def ring_last(state):
    back, ahead = state
    half = back.shape[1] // 2
    return shift(back[:, :half], "z", 1), shift(ahead[:, half:], "z", -1)


def add(a, b):
    return (a.astype(F32) + b.astype(F32)).astype(BF)


def scatter_first(blocks):
    own, to_m1, to_p1, to_m2, to_p2, to_m3, to_p3, to_4 = blocks
    half = own.shape[1] // 2
    right = shift(to_4[:, :half], "z", 1)
    left = shift(to_4[:, half:], "z", -1)
    right = jnp.concatenate([add(right, to_p3[:, :half]), to_p3[:, half:]], axis=1)
    left = jnp.concatenate([to_m3[:, :half], add(left, to_m3[:, half:])], axis=1)
    return right, left


def scatter_step(sums, right_term, left_term):
    right, left = sums
    return add(shift(right, "z", 1), right_term), add(shift(left, "z", -1), left_term)


def scatter_last(sums, own):
    right, left = sums
    right, left = shift(right, "z", 1), shift(left, "z", -1)
    return (right.astype(F32) + left.astype(F32) + own.astype(F32)).astype(BF)


def x_first(array):
    return shift(array, "x", 1), shift(array, "x", -1)


def x_second(before, ahead):
    half = before.shape[0] // 2
    return shift(before[:half], "x", 1), shift(ahead[half:], "x", -1)


def copies(plan, inputs, shapes):
    def kernel(*refs):
        pairs, chosen = plan(refs[: len(inputs)], refs[len(inputs) :])
        for a, b in pairs:
            b[...] = a[...]
        for when, a, b in chosen:

            @pl.when(when)
            def one_of():
                b[...] = a[...]

    return pl.pallas_call(
        kernel,
        out_shape=[jax.ShapeDtypeStruct(s, BF) for s in shapes],
        in_specs=[pl.BlockSpec(memory_space=pltpu.VMEM)] * len(inputs),
        out_specs=[pl.BlockSpec(memory_space=pltpu.VMEM)] * len(shapes),
        compiler_params=pltpu.CompilerParams(vmem_limit_bytes=24 * 2**20),
        cost_estimate=pl.CostEstimate(flops=0, bytes_accessed=0, transcendentals=0),
    )(*inputs)


def x_columns(width):
    return pl.ds(pl.multiple_of(lax.axis_index("x") * width, width), width)


def stack_rows(pieces, first, rows):
    width = pieces[0].shape[1]
    part = width // 4

    def plan(ins, outs):
        cut = pl.ds(first, rows)
        pairs = [(ins[i].at[cut], outs[0].at[pl.ds(rows * i, rows)]) for i in range(7)]
        for i in range(2):
            view = outs[0].at[pl.ds(rows * 7, rows), pl.ds(i * (width // 2), width // 2)]
            pairs.append((ins[7 + i].at[cut], view))
        x = lax.axis_index("x")
        own = x_columns(part)
        pairs += [(ins[i].at[cut, own], outs[1].at[pl.ds(rows * i, rows)]) for i in range(7)]
        at = pl.multiple_of(x % 2 * part, part)
        last = outs[1].at[pl.ds(rows * 7, rows)]
        return pairs, [(x // 2 == i, ins[7 + i].at[cut, pl.ds(at, part)], last) for i in range(2)]

    return copies(plan, pieces, [(8 * rows, width), (8 * rows, part)])


def stack_sources(pieces, rows):
    total, width = pieces[0].shape
    n = total // rows

    def plan(ins, outs):
        pairs = []
        for s in range(n):
            cut = pl.ds(s * rows, rows)
            for i in range(7):
                pairs.append((ins[i].at[cut], outs[0].at[s, pl.ds(rows * i, rows)]))
            for i in range(2):
                view = outs[0].at[s, pl.ds(rows * 7, rows), pl.ds(i * (width // 2), width // 2)]
                pairs.append((ins[7 + i].at[cut], view))
        return pairs, []

    return copies(plan, pieces, [(n, 8 * rows, width)])[0]


def merge_halves(own, other):
    rows, half = own.shape
    part = half // 4

    def plan(ins, outs):
        c = lax.axis_index("c")
        pairs = []
        for j in range(4):
            for ref, k in ((ins[0], c), (ins[1], 1 - c)):
                at = pl.multiple_of(j * 2 * part + k * part, part)
                pairs.append((ref.at[:, pl.ds(j * part, part)], outs[0].at[:, pl.ds(at, part)]))
        pairs.append((ins[1].at[:, x_columns(part)], outs[1]))
        return pairs, []

    return copies(plan, [own, other], [(rows, 2 * half), (rows, part)])


def split_halves(array):
    rows, width = array.shape
    part = width // 8

    def plan(ins, outs):
        c = lax.axis_index("c")
        pairs = []
        for j in range(4):
            for i, k in ((0, c), (1, 1 - c)):
                at = pl.multiple_of(j * 2 * part + k * part, part)
                pairs.append((ins[0].at[:, pl.ds(at, part)], outs[i].at[:, pl.ds(j * part, part)]))
        return pairs, []

    return copies(plan, [array], [(rows, width // 2)] * 2)


def dot(left, right, contract):
    return lax.dot_general(
        left, right, ((contract[:1], contract[1:]), ((), ())), preferred_element_type=F32
    )


def body(x_stash, x_scale, grad_out, w_gate, w_up, w_down):
    rows, width = x_stash.shape
    quarter = width // 8
    x, yh, c = lax.axis_index("x"), lax.axis_index("yh"), lax.axis_index("c")
    gate_t, up_t = w_gate.T, w_up.T
    inputs = (x_stash.astype(F32) * x_scale.astype(F32)[:, None]).astype(BF)

    def core_columns(array, core):
        at = [j * 2 * quarter + core * quarter for j in range(4)]
        return jnp.concatenate(
            [lax.dynamic_slice_in_dim(array, a, quarter, 1) for a in at], axis=1
        )

    pair = jnp.concatenate([inputs, grad_out], axis=0)
    mine, others = core_columns(pair, c), core_columns(pair, 1 - c)
    core = shift(others, "c", 1)
    along = shift(mine, "yl", 1)
    across = lax.ppermute(others, ("yl", "c"), [(0, 3), (1, 2), (2, 1), (3, 0)])
    ordered = [
        jnp.where(c == 0, mine, core),
        jnp.where(c == 0, core, mine),
        jnp.where(c == 0, along, across),
        jnp.where(c == 0, across, along),
    ]
    in_block = jnp.concatenate([a[:rows] for a in ordered], axis=0)
    go_block = jnp.concatenate([a[rows:] for a in ordered], axis=0)
    n = in_block.shape[0]

    both = jnp.concatenate([in_block, go_block], axis=0)
    far = [lax.dynamic_slice_in_dim(both, (x + by) % 4 * quarter, quarter, 1) for by in (1, 3, 2)]
    far = [shift(a, "x", by) for a, by in zip(far, (1, 3, 2))]

    state = (both, both)
    ring = [both]
    for step in range(3):
        state = ring_step(state)
        if step == 0:
            state, far = lax.optimization_barrier((state, far))
        ring += state
    far_block = jnp.concatenate(far, axis=0)
    last, far_1 = together(ring_last(state), ring_step((far_block, far_block)))
    ring += last
    in_own, in_cols = stack_rows(ring, 0, n)
    in_other = shift(in_own, "c", 1)
    go_own, go_cols = stack_rows(ring, n, n)
    go_other = shift(go_own, "c", 1)
    far_2 = ring_step(far_1)
    in_rows, in_cols_other = merge_halves(in_own, in_other)
    gate = dot(gate_t, in_rows, (1, 1))
    up = dot(up_t, in_rows, (1, 1))
    logistic = jax.nn.sigmoid(gate)
    swish = gate * logistic
    hidden = (swish * up).astype(BF)
    gate, up, hidden, go_own, go_other, far_2 = together(
        gate, up, hidden, go_own, go_other, far_2
    )
    far_3 = ring_step(far_2)
    go_rows, go_cols_other = merge_halves(go_own, go_other)
    grad_hidden = dot(w_down, go_rows, (1, 1))
    logistic = jax.nn.sigmoid(gate)
    swish = gate * logistic
    grad_up = (grad_hidden * swish).astype(BF)
    grad_gate = (grad_hidden * up * logistic * (1.0 + gate * (1.0 - logistic))).astype(BF)
    both = jnp.concatenate([grad_up, grad_gate], axis=0)
    both, grad_up, grad_gate, far_3, hidden = together(both, grad_up, grad_gate, far_3, hidden)

    both_1 = x_first(both)
    far_4 = ring_last(far_3)
    terms = (dot(grad_gate, gate_t, (0, 0)) + dot(grad_up, up_t, (0, 0))).astype(BF)
    mine, others = split_halves(terms)
    far_own = stack_sources([far_block, *far_1, *far_2, *far_3, *far_4], n)
    both, both_1, mine, others, far_own, hidden = together(
        both, both_1, mine, others, far_own, hidden
    )

    both_2 = x_second(*both_1)
    hidden_1 = x_first(hidden)
    far_other = shift(far_own, "c", 1)
    terms = add(mine, shift(others, "c", 1))
    blocks = [terms[i * n : (i + 1) * n] for i in range(8)]
    sums = scatter_first(blocks)
    both_2, hidden_1, far_other, sums = together(both_2, hidden_1, far_other, sums)

    def columns(own, far, i):
        return jnp.concatenate([own, far[i], far[2 + i], far[4 + i]], axis=0)

    def weight_terms(array, near, far, i, own, other):
        full = jnp.concatenate([array, *near, jnp.concatenate(far, axis=0)], axis=1)
        first = dot(full, columns(own, far_own, i), (1, 0)).astype(BF)
        second = dot(full, columns(other, far_other, i), (1, 0)).astype(BF)
        return jnp.where(c == yh, first, second), jnp.where(c == yh, second, first)

    ff = hidden.shape[0]
    sums = scatter_step(sums, blocks[4], blocks[3])
    kept, sent = weight_terms(both, both_1, both_2, 0, in_cols, in_cols_other)
    sent, hidden_1 = together(sent, hidden_1)
    got = shift(sent, "yh", 1)
    hidden_2 = x_second(*hidden_1)
    sums, hidden_2, sent = together(sums, hidden_2, sent)
    sums = scatter_step(sums, blocks[2], blocks[1])
    down_kept, down_sent = weight_terms(hidden, hidden_1, hidden_2, 1, go_cols, go_cols_other)
    down_got = shift(down_sent, "yh", 1)
    sums, down_sent = together(sums, down_sent)
    block = scatter_last(sums, blocks[0])
    block, got = together(block, got)
    up_grad, gate_grad = add(kept[:ff], got[:ff]), add(kept[ff:], got[ff:])
    half = n // 2
    block = block[:half].astype(F32) + shift(block[half:], "yl", 1).astype(F32)
    block = block.astype(BF)
    first, second = block[:rows], block[rows:]
    keep = jnp.where(c == 0, first, second)
    got = shift(jnp.where(c == 0, second, first), "c", 1)
    got, down_got = together(got, down_got)
    down = add(down_kept, down_got)
    low, high = jnp.where(c == 0, keep, got), jnp.where(c == 0, got, keep)
    parts = []
    for j in range(4):
        cut = slice(j * quarter, (j + 1) * quarter)
        parts += [low[:, cut], high[:, cut]]
    return jnp.concatenate(parts, axis=1), gate_grad.T, up_grad.T, down


def solution(mesh):
    fine = Mesh(mesh.devices.reshape(tuple(SIZES.values())), AXES)
    dp, tensor = ("x", "yh"), ("z", "yl", "c")
    return jax.shard_map(
        body,
        mesh=fine,
        in_specs=(
            P(AXES, None),
            P(AXES),
            P(AXES, None),
            P(None, tensor),
            P(None, tensor),
            P(tensor, None),
        ),
        out_specs=(P(AXES, None), P(dp, tensor), P(dp, tensor), P(tensor, dp)),
        check_vma=False,
    )
```
